32 devices in a mesh: layer: 2 (over core), blk: 16 (over z, y, x).
Axes of the slice: x: 2, y: 2, z: 4, core: 2. Of those that a mesh axis runs over, the one named last changes fastest.
Arguments:
- density: float32 [48, 6, 256, 256], P('blk'), may hold values from -0.15625 to 0.15625
- pattern: int32 [48, 6], replicated, may hold values from 0 to 47, as said below
Outputs:
- squared: float32 [48, 6, 256, 256], P('blk', None, None, 'layer')
- purified: float32 [48, 6, 256, 256], P('blk', None, None, 'layer')
The draws below stay inside these ranges and needn't reach their ends.
Inputs may be any that keep to these rules, and one draw needn't show every extreme that they name: pattern[i, 0] = i and pattern[i, 1 .. 5] = (i + d) mod 48 for 5 distinct nonzero offsets d in -3 .. 3.
All inputs are finite; a program needn't handle non-finite values.
Results may differ from the reference program's by a relative error of at most 0.0016.
Values may be sent and summed in bfloat16 or wider, within the bound.
A program may use at most 64 MiB of HBM per device.

```python
import jax
import jax.numpy as jnp
from jax import lax

BS = 256
K = 6
BAND = 3
NB = 48


def draw_pattern(key, part):
    rows = jnp.arange(NB, dtype=jnp.int32)
    dropped = jax.random.randint(key, (NB,), 0, 2 * BAND, dtype=jnp.int32)
    nonzero = jnp.concatenate([jnp.arange(-BAND, 0, dtype=jnp.int32), jnp.arange(1, BAND + 1, dtype=jnp.int32)])
    places = jnp.arange(K - 1, dtype=jnp.int32)
    index = places[None, :] + (places[None, :] >= dropped[:, None]).astype(jnp.int32)
    offsets = jnp.concatenate([jnp.zeros((NB, 1), jnp.int32), nonzero[index]], axis=1)
    return ((rows[:, None] + offsets) % NB).astype(jnp.int32)


def levels(own_key, dims, split, low, high):
    gain = 1.0
    for position, shards_of in split:
        draws = jax.random.uniform(jax.random.fold_in(jax.random.fold_in(own_key, 6), position), (shards_of,), jnp.float32, low / len(split), high / len(split))
        gain = gain * jnp.repeat(jnp.exp(draws), dims[position] // shards_of).reshape((-1,) + (1,) * (len(dims) - 1 - position))
    return gain


def bell_draw(own_key, dims, deviation, reach, split=(), kind=jnp.bfloat16):
    values = jax.random.normal(own_key, dims, jnp.float32) * deviation
    if len(split) > 0:
        values = levels(own_key, dims, split, -0.22, 0.18) * values
    return jnp.clip(values, min=-reach, max=reach).astype(kind)


def setup_inputs(seed: int = 0) -> dict:
    arg_keys = jax.random.split(jax.random.key(seed), 3)
    density = bell_draw(arg_keys[0], (NB, K, BS, BS), (K * BS) ** -0.5, 0.15625, ((0, 16),), jnp.float32)
    pattern = draw_pattern(jax.random.fold_in(arg_keys[2], 71), 0)
    return dict(density=density, pattern=pattern)


def reference(density, pattern):
    def one_row(i):
        own = pattern[i]
        neighbor = pattern[own]
        equal = neighbor[:, None, :] == own[None, :, None]
        slot = jnp.argmax(equal.astype(jnp.int32), axis=2).astype(jnp.int32)
        valid = jnp.any(equal, axis=2).astype(jnp.float32)
        picked = density[own[:, None], slot] * valid[:, :, None, None]
        left = density[i]
        squared = jnp.einsum('sac,stcb->tab', left, picked, precision=lax.Precision.HIGHEST)
        rounded = lax.optimization_barrier(squared.astype(jnp.bfloat16)).astype(jnp.float32)
        cubed = jnp.einsum('sac,stcb->tab', rounded, picked, precision=lax.Precision.HIGHEST)
        return squared, 3.0 * squared - 2.0 * cubed

    squared, purified = lax.map(one_row, jnp.arange(NB, dtype=jnp.int32))
    return (squared, purified)
```

```python
import jax
import jax.numpy as jnp
from jax import lax
from jax.experimental import pallas as pl
from jax.experimental.pallas import tpu as pltpu
from jax.sharding import PartitionSpec as P

BAND = 3
SPAN = 2 * BAND + 1
MESH = pl.DeviceIdType.MESH


def padded_2(value, sides, width):
    for axis, dim in sides:
        size, length = (lax.axis_size(axis), value.shape[dim])
        up = [(i, (i + 1) % size) for i in range(size)]
        down = [(j, i) for i, j in up]
        last = lax.slice_in_dim(value, length - width, length, axis=dim)
        initial = lax.slice_in_dim(value, 0, width, axis=dim)
        before = lax.ppermute(last, axis, up)
        after = lax.ppermute(initial, axis, down)
        value = jnp.concatenate([before, value, after], axis=dim)
    return value


def body(density, pattern):
    count_rows, slots, order, _ = density.shape
    width = order // lax.axis_size("layer")
    start_col = lax.axis_index("layer") * width
    total_rows = pattern.shape[0]
    first = lax.axis_index("blk") * count_rows
    own = lax.dynamic_slice_in_dim(pattern, first, count_rows, 0)
    neighbor = pattern[own]
    equal = neighbor[:, :, None, :] == own[:, None, :, None]
    slot = jnp.argmax(equal.astype(jnp.int32), axis=3)
    valid = jnp.any(equal, axis=3).astype(jnp.float32)
    row_ids = first + jnp.arange(count_rows, dtype=jnp.int32)
    offset = (own - row_ids[:, None] + BAND) % total_rows - BAND
    place = jnp.arange(count_rows, dtype=jnp.int32)[:, None] + BAND + offset
    col_part = lax.dynamic_slice_in_dim(density, start_col, width, 3)
    padded = padded_2(col_part, (("blk", 0),), BAND)
    highest = lax.Precision.HIGHEST
    picked = padded[place[:, :, None], slot] * valid[:, :, :, None, None]

    def product(left):
        return jnp.einsum("rsac,rstcb->rtab", left, picked, precision=highest)

    squared = product(density)
    rounded = squared.astype(jnp.bfloat16)
    cubed = product(lax.all_gather(rounded, "layer", axis=3, tiled=True).astype(jnp.float32))
    return (squared, 3.0 * squared - 2.0 * cubed)


def offsets_of(pattern_ref, row, total, slots):
    offs = []
    for u in range(slots):
        v = pattern_ref[row, u] - row
        v = jnp.where(v > BAND, v - total, v)
        v = jnp.where(v < -BAND, v + total, v)
        offs.append(v)
    return offs


def lacking(offs):
    s = offs[0]
    for v in offs[1:]:
        s = s + v
    return -s


def slot_of(offs, o):
    u = jnp.int32(0)
    for v in range(1, len(offs)):
        u = jnp.where(offs[v] == o, jnp.int32(v), u)
    return u


def step_kernel(pattern_ref, d_ref, sq_hbm, pu_hbm, own, xin, yin, zin, lhi, llo, phi, plo, acc, cub, sl,
                xs, xr, ys, yr, zs, zr, ss, sr, qs, us):
    rows, slots, order, _ = d_ref.shape
    total = pattern_ref.shape[0]
    half = order // 2
    layer = lax.axis_index("layer")
    b = lax.axis_index("blk")
    nb = lax.axis_size("blk")
    p = lax.rem(b, 4)
    x = lax.rem(p, 2)
    xb = b + 1 - 2 * x
    y = p // 2
    yb = b + 2 - 4 * y
    zup = lax.rem(b + 4, nb)
    zdn = lax.rem(b + nb - 4, nb)
    outer = (p == 0) | (p == 3)
    zt = jnp.where(p == 0, zup, zdn)
    first = b * rows
    bf = jnp.bfloat16
    f32 = jnp.float32

    barrier = pltpu.get_barrier_semaphore()
    for dev in ((layer, xb), (layer, yb), (layer, zup), (layer, zdn), (1 - layer, b)):
        pl.semaphore_signal(barrier, inc=1, device_id=dev, device_id_type=MESH)

    su = x
    ru = 1 - x

    def own_row(n):
        return jnp.where(su == 1, 2 - n, n)

    def x_copy(n, q):
        return (own.at[n, q], xin.at[n, q])

    relay = [(n, j) for n in range(3) for j in range(6 - n)]
    rest = [(1, 0), (2, 0), (2, 1)]

    def relay_place(flag, n, j):
        return jnp.where(flag == 1, n + j, j)

    def rest_place(flag, n, l):
        return jnp.where(flag == 1, l, 6 - n + l)

    def xsend(k):
        if k < 15:
            n, j = relay[k]
            q = relay_place(su, n, j)
        else:
            n, l = rest[k - 15]
            q = rest_place(su, n, l)
        return pltpu.make_async_remote_copy(
            src_ref=own.at[n, q], dst_ref=xin.at[n, q], send_sem=xs.at[k], recv_sem=xr.at[k],
            device_id=(layer, xb), device_id_type=MESH), n, q

    def xrecv(k):
        if k < 15:
            n, j = relay[k]
            q = relay_place(ru, n, j)
        else:
            n, l = rest[k - 15]
            q = rest_place(ru, n, l)
        return pltpu.make_async_remote_copy(
            src_ref=own.at[n, q], dst_ref=xin.at[n, q], send_sem=xs.at[k], recv_sem=xr.at[k],
            device_id=(layer, xb), device_id_type=MESH)

    def ycopy(k):
        n, j = relay[k]
        return pltpu.make_async_remote_copy(
            src_ref=xin.at[n, relay_place(ru, n, j)], dst_ref=yin.at[n, j], send_sem=ys.at[k], recv_sem=yr.at[k],
            device_id=(layer, yb), device_id_type=MESH)

    def zcopy(k):
        n, j = relay[k]
        return pltpu.make_async_remote_copy(
            src_ref=yin.at[n, j], dst_ref=zin.at[n, j], send_sem=zs.at[k], recv_sem=zr.at[k],
            device_id=(layer, zt), device_id_type=MESH)

    col = pl.multiple_of(layer * half, half)
    row_offs = [offsets_of(pattern_ref, first + m, total, slots) for m in range(rows)]
    row_lack = [lacking(o) for o in row_offs]

    sends = []
    for k in range(18):
        cp, n, q = xsend(k)
        m = own_row(n)
        offs = [jnp.where(su == 1, row_offs[2 - n][u], row_offs[n][u]) for u in range(slots)]
        lack = jnp.where(su == 1, row_lack[2 - n], row_lack[n])
        o = q - BAND
        o = jnp.where(o >= lack, o + 1, o)
        own[n, q] = d_ref[m, slot_of(offs, o), :, pl.ds(col, half)].astype(bf)
        if k == 0:
            pl.semaphore_wait(barrier, 5)
        cp.start()
        sends.append(cp)

    state = {"y": 0, "z": 0}

    def pump():
        k = state["y"]
        if k < 18:
            xrecv(k).wait_recv()
            if k < 15:
                ycopy(k).start()
            state["y"] = k + 1
        z = k - 1
        if 0 <= z < 15:
            ycopy(z).wait_recv()

            @pl.when(outer)
            def _():
                zcopy(z).start()

    def lay(m, q):
        offs = row_offs[m]
        here = (row_lack[m] != q - BAND).astype(f32)
        u = slot_of(offs, q - BAND)
        v = d_ref[m, u] * here
        hi = v.astype(bf)
        lhi[m, q] = hi
        llo[m, q] = (v - hi.astype(f32)).astype(bf)
        w = d_ref[m, u, :, pl.ds(col, half)] * here
        whi = w.astype(bf)
        phi[3 + m, q] = whi
        plo[m, q] = (w - whi.astype(f32)).astype(bf)

    for m in range(rows):
        for q in range(SPAN):
            lay(m, q)
        pump()

    def right(ref, k, d):
        lo, hi = max(0, -d), min(SPAN, SPAN - d)
        return jnp.concatenate([ref[k, q] for q in range(lo, hi)], axis=1), lo + d

    def add(target, i, value, e0):
        for c in range(value.shape[1] // half):
            target[i, e0 + c] += value[:, c * half:(c + 1) * half]

    def dot(a, c):
        return jnp.dot(a, c, preferred_element_type=f32)

    acc[...] = jnp.zeros_like(acc)
    cub[...] = jnp.zeros_like(cub)

    def local_square(i, m):
        d = m - i
        hi, e0 = right(phi, 3 + m, d)
        lo, _ = right(plo, m, d)
        a, a2 = lhi[i, d + BAND], llo[i, d + BAND]
        add(acc, i, dot(a, hi) + (dot(a2, hi) + dot(a, lo)), e0)

    def far_square(i, k):
        d = k - 3 - i
        hi, e0 = right(phi, k, d)
        add(acc, i, dot(lhi[i, d + BAND], hi) + dot(llo[i, d + BAND], hi), e0)

    for i in range(rows):
        for m in range(rows):
            local_square(i, m)
            pump()

    while state["y"] < 18:
        pump()

    def spread(side_up, get, n, m):
        k = (6 if side_up else 0) + m
        row = lax.rem(first + (rows if side_up else total - rows) + m, total)
        lack = lacking(offsets_of(pattern_ref, row, total, slots))
        lo, hi = (0, 6 - m) if side_up else (3 - m, SPAN)
        for q in range(lo, hi):
            o = q - BAND
            if q == 0:
                phi[k, q] = (get(n, 0).astype(f32) * (lack != o).astype(f32)).astype(bf)
                continue
            prev = get(n, q - 1).astype(f32) * (lack < o).astype(f32)
            if q < 6:
                prev = prev + get(n, q).astype(f32) * (lack > o).astype(f32)
            phi[k, q] = prev.astype(bf)

    @pl.when(x == 0)
    def _():
        for n in range(3):
            spread(True, lambda n, q: xin[n, q], n, 2 - n)

    @pl.when(x == 1)
    def _():
        for n in range(3):
            spread(False, lambda n, q: xin[n, q], n, n)

    @pl.when(outer)
    def _():
        for k in range(15):
            zcopy(k).wait_recv()

    for is_outer, ref in ((True, zin), (False, yin)):
        cond = outer if is_outer else jnp.logical_not(outer)

        @pl.when(cond & (x == 0))
        def _(ref=ref):
            for n in range(3):
                spread(False, lambda n, q: ref[n, q - n], n, 2 - n)

        @pl.when(cond & (x == 1))
        def _(ref=ref):
            for n in range(3):
                spread(True, lambda n, q: ref[n, q], n, n)

    scopies = []
    qcopies = []
    for i in range(rows):
        for k in list(range(i, 3)) + list(range(6, 7 + i)):
            far_square(i, k)
        for q in range(SPAN):
            here = (row_lack[i] != q - BAND).astype(f32)
            sl[layer, i, q] = (acc[i, q] * here).astype(bf)
        cp = pltpu.make_async_remote_copy(
            src_ref=sl.at[layer, i], dst_ref=sl.at[layer, i], send_sem=ss.at[i], recv_sem=sr.at[i],
            device_id=(1 - layer, b), device_id_type=MESH)
        cp.start()
        scopies.append(cp)
        cp = pltpu.make_async_copy(acc.at[i], sq_hbm.at[i], qs.at[i])
        cp.start()
        qcopies.append(cp)

    ucopies = []
    for i in range(rows):
        scopies[i].wait_send()
        pltpu.make_async_remote_copy(
            src_ref=sl.at[1 - layer, i], dst_ref=sl.at[1 - layer, i], send_sem=ss.at[i], recv_sem=sr.at[i],
            device_id=(1 - layer, b), device_id_type=MESH).wait_recv()
        for k in range(i, i + SPAN):
            d = k - 3 - i
            a = jnp.concatenate([sl[0, i, d + BAND], sl[1, i, d + BAND]], axis=1)
            hi, e0 = right(phi, k, d)
            v = dot(a, hi)
            if 3 <= k < 6:
                lo, _ = right(plo, k - 3, d)
                v = v + dot(a, lo)
            add(cub, i, v, e0)
        for q in range(SPAN):
            cub[i, q] = 3.0 * acc[i, q] - 2.0 * cub[i, q]
        cp = pltpu.make_async_copy(cub.at[i], pu_hbm.at[i], us.at[i])
        cp.start()
        ucopies.append(cp)

    for cp in sends:
        cp.wait_send()
    for k in range(15):
        ycopy(k).wait_send()

    @pl.when(outer)
    def _():
        for k in range(15):
            zcopy(k).wait_send()

    for cp in qcopies + ucopies:
        cp.wait()


def place_kernel(pattern_ref, sq, pu, sq_out, pu_out, sem):
    rows, slots = sq_out.shape[:2]
    total = pattern_ref.shape[0]
    first = lax.axis_index("blk") * rows
    copies = []
    for i in range(rows):
        offs = offsets_of(pattern_ref, first + i, total, slots)
        for t in range(slots):
            e = jnp.clip(offs[t] + BAND, 0, SPAN - 1)
            for a, (src, dst) in enumerate(((sq, sq_out), (pu, pu_out))):
                cp = pltpu.make_async_copy(src.at[i, e], dst.at[i, t], sem.at[a, i, t])
                cp.start()
                copies.append(cp)
    for cp in copies:
        cp.wait()


def fused(density, pattern):
    rows, slots, order, _ = density.shape
    half = order // 2
    dense = jax.ShapeDtypeStruct((rows, SPAN, order, half), jnp.float32)
    vmem, smem, anyspace = (pl.BlockSpec(memory_space=m) for m in (pltpu.VMEM, pltpu.SMEM, pl.ANY))
    bf, f32 = jnp.bfloat16, jnp.float32
    dma = pltpu.SemaphoreType.DMA
    block = (order, half)
    sq, pu = pl.pallas_call(
        step_kernel,
        out_shape=[dense, dense],
        in_specs=[smem, vmem],
        out_specs=[anyspace, anyspace],
        scratch_shapes=[
            pltpu.VMEM((3, 6) + block, bf),
            pltpu.VMEM((3, 6) + block, bf),
            pltpu.VMEM((3, 6) + block, bf),
            pltpu.VMEM((3, 6) + block, bf),
            pltpu.VMEM((rows, SPAN, order, order), bf),
            pltpu.VMEM((rows, SPAN, order, order), bf),
            pltpu.VMEM((9, SPAN) + block, bf),
            pltpu.VMEM((rows, SPAN) + block, bf),
            pltpu.VMEM((rows, SPAN) + block, f32),
            pltpu.VMEM((rows, SPAN) + block, f32),
            pltpu.VMEM((2, rows, SPAN) + block, bf),
            dma((18,)), dma((18,)), dma((15,)), dma((15,)), dma((15,)), dma((15,)),
            dma((3,)), dma((3,)), dma((3,)), dma((3,)),
        ],
        compiler_params=pltpu.CompilerParams(
            collective_id=0, has_side_effects=True, vmem_limit_bytes=56 * 1024 * 1024),
        cost_estimate=pl.CostEstimate(flops=10**10, bytes_accessed=10**7, transcendentals=0),
    )(pattern, density)
    out = jax.ShapeDtypeStruct((rows, slots, order, half), f32)
    return pl.pallas_call(
        place_kernel,
        out_shape=[out, out],
        in_specs=[smem, anyspace, anyspace],
        out_specs=[anyspace, anyspace],
        scratch_shapes=[dma((2, rows, slots))],
    )(pattern, sq, pu)


def solution(mesh):
    planes = mesh.shape["layer"] == 2 and mesh.shape["blk"] == 16
    return jax.shard_map(
        fused if planes else body,
        mesh=mesh,
        in_specs=(P("blk", None, None, None), P()),
        out_specs=(P("blk", None, None, "layer"), P("blk", None, None, "layer")),
        check_vma=False,
    )
```

```python
import jax
import jax.numpy as jnp
from jax import lax
from jax.experimental import pallas as pl
from jax.experimental.pallas import tpu as pltpu
from jax.sharding import PartitionSpec as P

BAND = 3
SPAN = 2 * BAND + 1
MESH = pl.DeviceIdType.MESH


def padded_2(value, sides, width):
    for axis, dim in sides:
        size, length = (lax.axis_size(axis), value.shape[dim])
        up = [(i, (i + 1) % size) for i in range(size)]
        down = [(j, i) for i, j in up]
        last = lax.slice_in_dim(value, length - width, length, axis=dim)
        initial = lax.slice_in_dim(value, 0, width, axis=dim)
        before = lax.ppermute(last, axis, up)
        after = lax.ppermute(initial, axis, down)
        value = jnp.concatenate([before, value, after], axis=dim)
    return value


def body(density, pattern):
    count_rows, slots, order, _ = density.shape
    width = order // lax.axis_size("layer")
    start_col = lax.axis_index("layer") * width
    total_rows = pattern.shape[0]
    first = lax.axis_index("blk") * count_rows
    own = lax.dynamic_slice_in_dim(pattern, first, count_rows, 0)
    neighbor = pattern[own]
    equal = neighbor[:, :, None, :] == own[:, None, :, None]
    slot = jnp.argmax(equal.astype(jnp.int32), axis=3)
    valid = jnp.any(equal, axis=3).astype(jnp.float32)
    row_ids = first + jnp.arange(count_rows, dtype=jnp.int32)
    offset = (own - row_ids[:, None] + BAND) % total_rows - BAND
    place = jnp.arange(count_rows, dtype=jnp.int32)[:, None] + BAND + offset
    col_part = lax.dynamic_slice_in_dim(density, start_col, width, 3)
    padded = padded_2(col_part, (("blk", 0),), BAND)
    highest = lax.Precision.HIGHEST
    picked = padded[place[:, :, None], slot] * valid[:, :, :, None, None]

    def product(left):
        return jnp.einsum("rsac,rstcb->rtab", left, picked, precision=highest)

    squared = product(density)
    rounded = squared.astype(jnp.bfloat16)
    cubed = product(lax.all_gather(rounded, "layer", axis=3, tiled=True).astype(jnp.float32))
    return (squared, 3.0 * squared - 2.0 * cubed)


def offsets_of(pattern_ref, row, total, slots):
    offs = []
    for u in range(slots):
        v = pattern_ref[row, u] - row
        v = jnp.where(v > BAND, v - total, v)
        v = jnp.where(v < -BAND, v + total, v)
        offs.append(v)
    return offs


def lacking(offs):
    s = offs[0]
    for v in offs[1:]:
        s = s + v
    return -s


def slot_of(offs, o):
    u = jnp.int32(0)
    for v in range(1, len(offs)):
        u = jnp.where(offs[v] == o, jnp.int32(v), u)
    return u


def step_kernel(pattern_ref, d_ref, acc, cub, own, xin, yin, zin, lhi, llo, phi, plo, sl,
                xs, xr, ys, yr, zs, zr, ss, sr):
    rows, slots, order, _ = d_ref.shape
    total = pattern_ref.shape[0]
    half = order // 2
    layer = lax.axis_index("layer")
    b = lax.axis_index("blk")
    nb = lax.axis_size("blk")
    p = lax.rem(b, 4)
    x = lax.rem(p, 2)
    xb = b + 1 - 2 * x
    y = p // 2
    yb = b + 2 - 4 * y
    zup = lax.rem(b + 4, nb)
    zdn = lax.rem(b + nb - 4, nb)
    outer = (p == 0) | (p == 3)
    zt = jnp.where(p == 0, zup, zdn)
    first = b * rows
    bf = jnp.bfloat16
    f32 = jnp.float32

    barrier = pltpu.get_barrier_semaphore()
    for dev in ((layer, xb), (layer, yb), (layer, zup), (layer, zdn), (1 - layer, b)):
        pl.semaphore_signal(barrier, inc=1, device_id=dev, device_id_type=MESH)

    su = x
    ru = 1 - x

    def own_row(n):
        return jnp.where(su == 1, 2 - n, n)

    def x_copy(n, q):
        return (own.at[n, q], xin.at[n, q])

    relay = [(n, j) for n in range(3) for j in range(6 - n)]
    rest = [(1, 0), (2, 0), (2, 1)]

    def relay_place(flag, n, j):
        return jnp.where(flag == 1, n + j, j)

    def rest_place(flag, n, l):
        return jnp.where(flag == 1, l, 6 - n + l)

    def xsend(k):
        if k < 15:
            n, j = relay[k]
            q = relay_place(su, n, j)
        else:
            n, l = rest[k - 15]
            q = rest_place(su, n, l)
        return pltpu.make_async_remote_copy(
            src_ref=own.at[n, q], dst_ref=xin.at[n, q], send_sem=xs.at[k], recv_sem=xr.at[k],
            device_id=(layer, xb), device_id_type=MESH), n, q

    def xrecv(k):
        if k < 15:
            n, j = relay[k]
            q = relay_place(ru, n, j)
        else:
            n, l = rest[k - 15]
            q = rest_place(ru, n, l)
        return pltpu.make_async_remote_copy(
            src_ref=own.at[n, q], dst_ref=xin.at[n, q], send_sem=xs.at[k], recv_sem=xr.at[k],
            device_id=(layer, xb), device_id_type=MESH)

    def ycopy(k):
        n, j = relay[k]
        return pltpu.make_async_remote_copy(
            src_ref=xin.at[n, relay_place(ru, n, j)], dst_ref=yin.at[n, j], send_sem=ys.at[k], recv_sem=yr.at[k],
            device_id=(layer, yb), device_id_type=MESH)

    def zcopy(k):
        n, j = relay[k]
        return pltpu.make_async_remote_copy(
            src_ref=yin.at[n, j], dst_ref=zin.at[n, j], send_sem=zs.at[k], recv_sem=zr.at[k],
            device_id=(layer, zt), device_id_type=MESH)

    col = pl.multiple_of(layer * half, half)
    row_offs = [offsets_of(pattern_ref, first + m, total, slots) for m in range(rows)]
    row_lack = [lacking(o) for o in row_offs]

    sends = []
    for k in range(18):
        cp, n, q = xsend(k)
        m = own_row(n)
        offs = [jnp.where(su == 1, row_offs[2 - n][u], row_offs[n][u]) for u in range(slots)]
        lack = jnp.where(su == 1, row_lack[2 - n], row_lack[n])
        o = q - BAND
        o = jnp.where(o >= lack, o + 1, o)
        own[n, q] = d_ref[m, slot_of(offs, o), :, pl.ds(col, half)].astype(bf)
        if k == 0:
            pl.semaphore_wait(barrier, 5)
        cp.start()
        sends.append(cp)

    state = {"y": 0, "z": 0}

    def pump():
        k = state["y"]
        if k < 18:
            xrecv(k).wait_recv()
            if k < 15:
                ycopy(k).start()
            state["y"] = k + 1
        z = k - 1
        if 0 <= z < 15:
            ycopy(z).wait_recv()

            @pl.when(outer)
            def _():
                zcopy(z).start()

    def lay(m, q):
        offs = row_offs[m]
        here = (row_lack[m] != q - BAND).astype(f32)
        u = slot_of(offs, q - BAND)
        v = d_ref[m, u] * here
        hi = v.astype(bf)
        lhi[m, q] = hi
        llo[m, q] = (v - hi.astype(f32)).astype(bf)
        w = d_ref[m, u, :, pl.ds(col, half)] * here
        whi = w.astype(bf)
        phi[3 + m, q] = whi
        plo[m, q] = (w - whi.astype(f32)).astype(bf)

    for m in range(rows):
        for q in range(SPAN):
            lay(m, q)
        pump()

    def right(ref, k, d):
        lo, hi = max(0, -d), min(SPAN, SPAN - d)
        return jnp.concatenate([ref[k, q] for q in range(lo, hi)], axis=1), lo + d

    def add(target, i, value, e0):
        for c in range(value.shape[1] // half):
            target[i, e0 + c] += value[:, c * half:(c + 1) * half]

    def dot(a, c):
        return jnp.dot(a, c, preferred_element_type=f32)

    acc[...] = jnp.zeros_like(acc)
    cub[...] = jnp.zeros_like(cub)

    def local_square(i, m):
        d = m - i
        hi, e0 = right(phi, 3 + m, d)
        lo, _ = right(plo, m, d)
        a, a2 = lhi[i, d + BAND], llo[i, d + BAND]
        add(acc, i, dot(a, hi) + (dot(a2, hi) + dot(a, lo)), e0)

    def far_square(i, k):
        d = k - 3 - i
        hi, e0 = right(phi, k, d)
        add(acc, i, dot(lhi[i, d + BAND], hi) + dot(llo[i, d + BAND], hi), e0)

    for i in range(rows):
        for m in range(rows):
            local_square(i, m)
            pump()

    while state["y"] < 18:
        pump()

    def spread(side_up, get, n, m):
        k = (6 if side_up else 0) + m
        row = lax.rem(first + (rows if side_up else total - rows) + m, total)
        lack = lacking(offsets_of(pattern_ref, row, total, slots))
        lo, hi = (0, 6 - m) if side_up else (3 - m, SPAN)
        for q in range(lo, hi):
            o = q - BAND
            if q == 0:
                phi[k, q] = (get(n, 0).astype(f32) * (lack != o).astype(f32)).astype(bf)
                continue
            prev = get(n, q - 1).astype(f32) * (lack < o).astype(f32)
            if q < 6:
                prev = prev + get(n, q).astype(f32) * (lack > o).astype(f32)
            phi[k, q] = prev.astype(bf)

    @pl.when(x == 0)
    def _():
        for n in range(3):
            spread(True, lambda n, q: xin[n, q], n, 2 - n)

    @pl.when(x == 1)
    def _():
        for n in range(3):
            spread(False, lambda n, q: xin[n, q], n, n)

    @pl.when(outer)
    def _():
        for k in range(15):
            zcopy(k).wait_recv()

    for is_outer, ref in ((True, zin), (False, yin)):
        cond = outer if is_outer else jnp.logical_not(outer)

        @pl.when(cond & (x == 0))
        def _(ref=ref):
            for n in range(3):
                spread(False, lambda n, q: ref[n, q - n], n, 2 - n)

        @pl.when(cond & (x == 1))
        def _(ref=ref):
            for n in range(3):
                spread(True, lambda n, q: ref[n, q], n, n)

    scopies = []
    for i in range(rows):
        for k in list(range(i, 3)) + list(range(6, 7 + i)):
            far_square(i, k)
        for q in range(SPAN):
            here = (row_lack[i] != q - BAND).astype(f32)
            sl[layer, i, q] = (acc[i, q] * here).astype(bf)
        cp = pltpu.make_async_remote_copy(
            src_ref=sl.at[layer, i], dst_ref=sl.at[layer, i], send_sem=ss.at[i], recv_sem=sr.at[i],
            device_id=(1 - layer, b), device_id_type=MESH)
        cp.start()
        scopies.append(cp)

    for i in range(rows):
        scopies[i].wait_send()
        pltpu.make_async_remote_copy(
            src_ref=sl.at[1 - layer, i], dst_ref=sl.at[1 - layer, i], send_sem=ss.at[i], recv_sem=sr.at[i],
            device_id=(1 - layer, b), device_id_type=MESH).wait_recv()
        for k in range(i, i + SPAN):
            d = k - 3 - i
            a = jnp.concatenate([sl[0, i, d + BAND], sl[1, i, d + BAND]], axis=1)
            hi, e0 = right(phi, k, d)
            v = dot(a, hi)
            if 3 <= k < 6:
                lo, _ = right(plo, k - 3, d)
                v = v + dot(a, lo)
            add(cub, i, v, e0)
        for q in range(SPAN):
            cub[i, q] = 3.0 * acc[i, q] - 2.0 * cub[i, q]

    for cp in sends:
        cp.wait_send()
    for k in range(15):
        ycopy(k).wait_send()

    @pl.when(outer)
    def _():
        for k in range(15):
            zcopy(k).wait_send()


def place_kernel(pattern_ref, sq, pu, sq_out, pu_out, sem):
    rows, slots = sq_out.shape[:2]
    total = pattern_ref.shape[0]
    first = lax.axis_index("blk") * rows
    copies = []
    for i in range(rows):
        offs = offsets_of(pattern_ref, first + i, total, slots)
        for t in range(slots):
            e = jnp.clip(offs[t] + BAND, 0, SPAN - 1)
            for a, (src, dst) in enumerate(((sq, sq_out), (pu, pu_out))):
                cp = pltpu.make_async_copy(src.at[i, e], dst.at[i, t], sem.at[a, i, t])
                cp.start()
                copies.append(cp)
    for cp in copies:
        cp.wait()


def fused(density, pattern):
    rows, slots, order, _ = density.shape
    half = order // 2
    dense = pltpu.VMEM((rows, SPAN, order, half), jnp.float32)
    vmem, smem, anyspace = (pl.BlockSpec(memory_space=m) for m in (pltpu.VMEM, pltpu.SMEM, pl.ANY))
    bf, f32 = jnp.bfloat16, jnp.float32
    dma = pltpu.SemaphoreType.DMA
    block = (order, half)
    sq, pu = pl.pallas_call(
        step_kernel,
        out_shape=[dense, dense],
        in_specs=[smem, vmem],
        out_specs=[vmem, vmem],
        scratch_shapes=[
            pltpu.VMEM((3, 6) + block, bf),
            pltpu.VMEM((3, 6) + block, bf),
            pltpu.VMEM((3, 6) + block, bf),
            pltpu.VMEM((3, 6) + block, bf),
            pltpu.VMEM((rows, SPAN, order, order), bf),
            pltpu.VMEM((rows, SPAN, order, order), bf),
            pltpu.VMEM((9, SPAN) + block, bf),
            pltpu.VMEM((rows, SPAN) + block, bf),
            pltpu.VMEM((2, rows, SPAN) + block, bf),
            dma((18,)), dma((18,)), dma((15,)), dma((15,)), dma((15,)), dma((15,)),
            dma((3,)), dma((3,)),
        ],
        compiler_params=pltpu.CompilerParams(
            collective_id=0, has_side_effects=True, vmem_limit_bytes=40 * 1024 * 1024),
        cost_estimate=pl.CostEstimate(flops=10**10, bytes_accessed=10**7, transcendentals=0),
    )(pattern, density)
    out = jax.ShapeDtypeStruct((rows, slots, order, half), f32)
    return pl.pallas_call(
        place_kernel,
        out_shape=[out, out],
        in_specs=[smem, vmem, vmem],
        out_specs=[anyspace, anyspace],
        scratch_shapes=[dma((2, rows, slots))],
    )(pattern, sq, pu)


def solution(mesh):
    planes = mesh.shape["layer"] == 2 and mesh.shape["blk"] == 16
    return jax.shard_map(
        fused if planes else body,
        mesh=mesh,
        in_specs=(P("blk", None, None, None), P()),
        out_specs=(P("blk", None, None, "layer"), P("blk", None, None, "layer")),
        check_vma=False,
    )
```

```python
import jax
import jax.numpy as jnp
from jax import lax
from jax.experimental import pallas as pl
from jax.experimental.pallas import tpu as pltpu
from jax.sharding import PartitionSpec as P

BAND = 3
SPAN = 2 * BAND + 1
MESH = pl.DeviceIdType.MESH


def padded_2(value, sides, width):
    for axis, dim in sides:
        size, length = (lax.axis_size(axis), value.shape[dim])
        up = [(i, (i + 1) % size) for i in range(size)]
        down = [(j, i) for i, j in up]
        last = lax.slice_in_dim(value, length - width, length, axis=dim)
        initial = lax.slice_in_dim(value, 0, width, axis=dim)
        before = lax.ppermute(last, axis, up)
        after = lax.ppermute(initial, axis, down)
        value = jnp.concatenate([before, value, after], axis=dim)
    return value


def body(density, pattern):
    count_rows, slots, order, _ = density.shape
    width = order // lax.axis_size("layer")
    start_col = lax.axis_index("layer") * width
    total_rows = pattern.shape[0]
    first = lax.axis_index("blk") * count_rows
    own = lax.dynamic_slice_in_dim(pattern, first, count_rows, 0)
    neighbor = pattern[own]
    equal = neighbor[:, :, None, :] == own[:, None, :, None]
    slot = jnp.argmax(equal.astype(jnp.int32), axis=3)
    valid = jnp.any(equal, axis=3).astype(jnp.float32)
    row_ids = first + jnp.arange(count_rows, dtype=jnp.int32)
    offset = (own - row_ids[:, None] + BAND) % total_rows - BAND
    place = jnp.arange(count_rows, dtype=jnp.int32)[:, None] + BAND + offset
    col_part = lax.dynamic_slice_in_dim(density, start_col, width, 3)
    padded = padded_2(col_part, (("blk", 0),), BAND)
    highest = lax.Precision.HIGHEST
    picked = padded[place[:, :, None], slot] * valid[:, :, :, None, None]

    def product(left):
        return jnp.einsum("rsac,rstcb->rtab", left, picked, precision=highest)

    squared = product(density)
    rounded = squared.astype(jnp.bfloat16)
    cubed = product(lax.all_gather(rounded, "layer", axis=3, tiled=True).astype(jnp.float32))
    return (squared, 3.0 * squared - 2.0 * cubed)


def offsets_of(pattern_ref, row, total, slots):
    offs = []
    for u in range(slots):
        v = pattern_ref[row, u] - row
        v = jnp.where(v > BAND, v - total, v)
        v = jnp.where(v < -BAND, v + total, v)
        offs.append(v)
    return offs


def lacking(offs):
    s = offs[0]
    for v in offs[1:]:
        s = s + v
    return -s


def slot_of(offs, o):
    u = jnp.int32(0)
    for v in range(1, len(offs)):
        u = jnp.where(offs[v] == o, jnp.int32(v), u)
    return u


def step_kernel(pattern_ref, d_hbm, acc, cub, d0, d1, d2, own, xin, yin, zin, lhi, llo, phi, plo, sl,
                xs, xr, ys, yr, zs, zr, ss, sr, ds):
    rows, slots, order, _ = d_hbm.shape
    total = pattern_ref.shape[0]
    half = order // 2
    layer = lax.axis_index("layer")
    b = lax.axis_index("blk")
    nb = lax.axis_size("blk")
    p = lax.rem(b, 4)
    x = lax.rem(p, 2)
    xb = b + 1 - 2 * x
    y = p // 2
    yb = b + 2 - 4 * y
    zup = lax.rem(b + 4, nb)
    zdn = lax.rem(b + nb - 4, nb)
    outer = (p == 0) | (p == 3)
    zt = jnp.where(p == 0, zup, zdn)
    first = b * rows
    bf = jnp.bfloat16
    f32 = jnp.float32

    barrier = pltpu.get_barrier_semaphore()
    for dev in ((layer, xb), (layer, yb), (layer, zup), (layer, zdn), (1 - layer, b)):
        pl.semaphore_signal(barrier, inc=1, device_id=dev, device_id_type=MESH)

    su = x
    ru = 1 - x

    def own_row(n):
        return jnp.where(su == 1, 2 - n, n)

    held = (d0, d1, d2)
    loads = [pltpu.make_async_copy(d_hbm.at[own_row(n)], held[n], ds.at[n]) for n in range(3)]
    for cp in loads:
        cp.start()

    relay = [(n, j) for n in range(3) for j in range(6 - n)]
    rest = [(1, 0), (2, 0), (2, 1)]

    def relay_place(flag, n, j):
        return jnp.where(flag == 1, n + j, j)

    def rest_place(flag, n, l):
        return jnp.where(flag == 1, l, 6 - n + l)

    def xsend(k):
        if k < 15:
            n, j = relay[k]
            q = relay_place(su, n, j)
        else:
            n, l = rest[k - 15]
            q = rest_place(su, n, l)
        return pltpu.make_async_remote_copy(
            src_ref=own.at[n, q], dst_ref=xin.at[n, q], send_sem=xs.at[k], recv_sem=xr.at[k],
            device_id=(layer, xb), device_id_type=MESH), n, q

    def xrecv(k):
        if k < 15:
            n, j = relay[k]
            q = relay_place(ru, n, j)
        else:
            n, l = rest[k - 15]
            q = rest_place(ru, n, l)
        return pltpu.make_async_remote_copy(
            src_ref=own.at[n, q], dst_ref=xin.at[n, q], send_sem=xs.at[k], recv_sem=xr.at[k],
            device_id=(layer, xb), device_id_type=MESH)

    def ycopy(k):
        n, j = relay[k]
        return pltpu.make_async_remote_copy(
            src_ref=xin.at[n, relay_place(ru, n, j)], dst_ref=yin.at[n, j], send_sem=ys.at[k], recv_sem=yr.at[k],
            device_id=(layer, yb), device_id_type=MESH)

    def zcopy(k):
        n, j = relay[k]
        return pltpu.make_async_remote_copy(
            src_ref=yin.at[n, j], dst_ref=zin.at[n, j], send_sem=zs.at[k], recv_sem=zr.at[k],
            device_id=(layer, zt), device_id_type=MESH)

    col = pl.multiple_of(layer * half, half)
    row_offs = [offsets_of(pattern_ref, first + m, total, slots) for m in range(rows)]
    row_lack = [lacking(o) for o in row_offs]

    sends = []
    by_n = []
    for n in range(3):
        offs = [jnp.where(su == 1, row_offs[2 - n][u], row_offs[n][u]) for u in range(slots)]
        by_n.append((offs, jnp.where(su == 1, row_lack[2 - n], row_lack[n])))
    for k in range(18):
        cp, n, q = xsend(k)
        offs, lack = by_n[n]
        if k in (0, 6, 11):
            loads[n].wait()
        o = q - BAND
        o = jnp.where(o >= lack, o + 1, o)
        own[n, q] = held[n][slot_of(offs, o), :, pl.ds(col, half)].astype(bf)
        if k == 0:
            pl.semaphore_wait(barrier, 5)
        cp.start()
        sends.append(cp)

    state = {"y": 0, "z": 0}

    def pump():
        k = state["y"]
        if k < 18:
            xrecv(k).wait_recv()
            if k < 15:
                ycopy(k).start()
            state["y"] = k + 1
        z = k - 1
        if 0 <= z < 15:
            ycopy(z).wait_recv()

            @pl.when(outer)
            def _():
                zcopy(z).start()

    def lay(n, q):
        offs, lack = by_n[n]
        m = own_row(n)
        here = (lack != q - BAND).astype(f32)
        u = slot_of(offs, q - BAND)
        v = held[n][u] * here
        hi = v.astype(bf)
        lhi[m, q] = hi
        llo[m, q] = (v - hi.astype(f32)).astype(bf)
        w = held[n][u, :, pl.ds(col, half)] * here
        whi = w.astype(bf)
        phi[3 + m, q] = whi
        plo[m, q] = (w - whi.astype(f32)).astype(bf)

    for n in range(rows):
        for q in range(SPAN):
            lay(n, q)
            if q in (3, 6):
                pump()

    def right(ref, k, d):
        lo, hi = max(0, -d), min(SPAN, SPAN - d)
        return jnp.concatenate([ref[k, q] for q in range(lo, hi)], axis=1), lo + d

    def add(target, i, value, e0):
        for c in range(value.shape[1] // half):
            target[i, e0 + c] += value[:, c * half:(c + 1) * half]

    def dot(a, c):
        return jnp.dot(a, c, preferred_element_type=f32)

    acc[...] = jnp.zeros_like(acc)
    cub[...] = jnp.zeros_like(cub)

    def local_square(i, m):
        d = m - i
        hi, e0 = right(phi, 3 + m, d)
        lo, _ = right(plo, m, d)
        a, a2 = lhi[i, d + BAND], llo[i, d + BAND]
        add(acc, i, dot(a, hi) + (dot(a2, hi) + dot(a, lo)), e0)

    def far_square(i, k):
        d = k - 3 - i
        hi, e0 = right(phi, k, d)
        add(acc, i, dot(lhi[i, d + BAND], hi) + dot(llo[i, d + BAND], hi), e0)

    def spread(side_up, get, n, m):
        k = (6 if side_up else 0) + m
        row = lax.rem(first + (rows if side_up else total - rows) + m, total)
        lack = lacking(offsets_of(pattern_ref, row, total, slots))
        lo, hi = (0, 6 - m) if side_up else (3 - m, SPAN)
        for q in range(lo, hi):
            o = q - BAND
            if q == 0:
                phi[k, q] = (get(n, 0).astype(f32) * (lack != o).astype(f32)).astype(bf)
                continue
            prev = get(n, q - 1).astype(f32) * (lack < o).astype(f32)
            if q < 6:
                prev = prev + get(n, q).astype(f32) * (lack > o).astype(f32)
            phi[k, q] = prev.astype(bf)

    def by_side(step):
        for side in (0, 1):
            @pl.when(x == side)
            def _(side=side):
                step(side)

    def x_row(n):
        def step(side):
            m = n if side else 2 - n
            spread(side == 0, lambda n, q: xin[n, q], n, m)
            if side:
                for i in range(n + 1):
                    far_square(i, n)
            else:
                for i in range(2 - n, rows):
                    far_square(i, 8 - n)
        by_side(step)

    def w_row(n):
        span = range(*((0, 6), (6, 11), (11, 15))[n])

        @pl.when(outer)
        def _():
            for k in span:
                zcopy(k).wait_recv()

        def step(side):
            m = n if side else 2 - n
            for ref, cond in ((zin, outer), (yin, jnp.logical_not(outer))):
                @pl.when(cond)
                def _(ref=ref):
                    if side:
                        spread(True, lambda n, q: ref[n, q], n, n)
                    else:
                        spread(False, lambda n, q: ref[n, q - n], n, 2 - n)
            if side:
                for i in range(n, rows):
                    far_square(i, 6 + n)
            else:
                for i in range(3 - n):
                    far_square(i, 2 - n)
        by_side(step)

    def row_at(j):
        return jnp.where(x == 1, j, 2 - j)

    def swap(j):
        i = row_at(j)
        return pltpu.make_async_remote_copy(
            src_ref=sl.at[layer, i], dst_ref=sl.at[layer, i], send_sem=ss.at[j], recv_sem=sr.at[j],
            device_id=(1 - layer, b), device_id_type=MESH)

    def swap_in(j):
        i = row_at(j)
        return pltpu.make_async_remote_copy(
            src_ref=sl.at[1 - layer, i], dst_ref=sl.at[1 - layer, i], send_sem=ss.at[j], recv_sem=sr.at[j],
            device_id=(1 - layer, b), device_id_type=MESH)

    def share(j):
        def step(side):
            i = j if side else 2 - j
            for q in range(SPAN):
                here = (row_lack[i] != q - BAND).astype(f32)
                sl[layer, i, q] = (acc[i, q] * here).astype(bf)
        by_side(step)
        swap(j).start()

    def cube(j):
        swap_in(j).wait_recv()

        def step(side):
            i = j if side else 2 - j
            for k in range(i, i + SPAN):
                d = k - 3 - i
                a = jnp.concatenate([sl[0, i, d + BAND], sl[1, i, d + BAND]], axis=1)
                hi, e0 = right(phi, k, d)
                v = dot(a, hi)
                if 3 <= k < 6:
                    lo, _ = right(plo, k - 3, d)
                    v = v + dot(a, lo)
                add(cub, i, v, e0)
            for q in range(SPAN):
                cub[i, q] = 3.0 * acc[i, q] - 2.0 * cub[i, q]
        by_side(step)

    for i in range(rows):
        for m in range(rows):
            local_square(i, m)
            if state["y"] < 14:
                pump()
    while state["y"] < 14:
        pump()
    x_row(0)
    pump()
    w_row(0)
    pump()
    pump()
    x_row(1)
    pump()
    w_row(1)
    while state["y"] < 18:
        pump()
    x_row(2)
    share(0)
    share(1)
    cube(0)
    w_row(2)
    share(2)
    cube(1)
    cube(2)
    for j in range(rows):
        swap(j).wait_send()

    for cp in sends:
        cp.wait_send()
    for k in range(15):
        ycopy(k).wait_send()

    @pl.when(outer)
    def _():
        for k in range(15):
            zcopy(k).wait_send()


def place_kernel(pattern_ref, sq, pu, sq_out, pu_out, sem):
    rows, slots = sq_out.shape[:2]
    total = pattern_ref.shape[0]
    first = lax.axis_index("blk") * rows
    copies = []
    for i in range(rows):
        offs = offsets_of(pattern_ref, first + i, total, slots)
        for t in range(slots):
            e = jnp.clip(offs[t] + BAND, 0, SPAN - 1)
            for a, (src, dst) in enumerate(((sq, sq_out), (pu, pu_out))):
                cp = pltpu.make_async_copy(src.at[i, e], dst.at[i, t], sem.at[a, i, t])
                cp.start()
                copies.append(cp)
    for cp in copies:
        cp.wait()


def fused(density, pattern):
    rows, slots, order, _ = density.shape
    half = order // 2
    dense = pltpu.VMEM((rows, SPAN, order, half), jnp.float32)
    vmem, smem, hbm = (pl.BlockSpec(memory_space=m) for m in (pltpu.VMEM, pltpu.SMEM, pltpu.HBM))
    bf, f32 = jnp.bfloat16, jnp.float32
    dma = pltpu.SemaphoreType.DMA
    block = (order, half)
    sq, pu = pl.pallas_call(
        step_kernel,
        out_shape=[dense, dense],
        in_specs=[smem, hbm],
        out_specs=[vmem, vmem],
        scratch_shapes=[
            pltpu.VMEM((slots, order, order), f32),
            pltpu.VMEM((slots, order, order), f32),
            pltpu.VMEM((slots, order, order), f32),
            pltpu.VMEM((3, 6) + block, bf),
            pltpu.VMEM((3, 6) + block, bf),
            pltpu.VMEM((3, 6) + block, bf),
            pltpu.VMEM((3, 6) + block, bf),
            pltpu.VMEM((rows, SPAN, order, order), bf),
            pltpu.VMEM((rows, SPAN, order, order), bf),
            pltpu.VMEM((9, SPAN) + block, bf),
            pltpu.VMEM((rows, SPAN) + block, bf),
            pltpu.VMEM((2, rows, SPAN) + block, bf),
            dma((18,)), dma((18,)), dma((15,)), dma((15,)), dma((15,)), dma((15,)),
            dma((3,)), dma((3,)), dma((3,)),
        ],
        compiler_params=pltpu.CompilerParams(
            collective_id=0, has_side_effects=True, vmem_limit_bytes=40 * 1024 * 1024),
        cost_estimate=pl.CostEstimate(flops=10**10, bytes_accessed=10**7, transcendentals=0),
    )(pattern, density)
    out = jax.ShapeDtypeStruct((rows, slots, order, half), f32)
    return pl.pallas_call(
        place_kernel,
        out_shape=[out, out],
        in_specs=[smem, vmem, vmem],
        out_specs=[hbm, hbm],
        scratch_shapes=[dma((2, rows, slots))],
        compiler_params=pltpu.CompilerParams(vmem_limit_bytes=4 * 1024 * 1024),
    )(pattern, sq, pu)


def solution(mesh):
    planes = mesh.shape["layer"] == 2 and mesh.shape["blk"] == 16
    return jax.shard_map(
        fused if planes else body,
        mesh=mesh,
        in_specs=(P("blk", None, None, None), P()),
        out_specs=(P("blk", None, None, "layer"), P("blk", None, None, "layer")),
        check_vma=False,
    )
```
